32 devices in a mesh: gx: 4 (over y, core), gy: 4 (over z), pa: 2 (over x).
Axes of the slice: x: 2, y: 2, z: 4, core: 2. Of those that a mesh axis runs over, the one named last changes fastest.
Arguments:
- volume: bfloat16 [4, 2048, 1024], P('pa', 'gx', 'gy'), may hold values from -6 to 6
- view_slopes: int32 [2, 16], replicated, may hold values from -14 to 14, as said below
- measured_x: float32 [16, 4, 1024], P(None, 'pa', 'gy'), may hold values from -6 to 6
- measured_y: float32 [16, 4, 2048], P(None, 'pa', 'gx'), may hold values from -6 to 6
Outputs:
- gradient: float32 [4, 2048, 1024], P('pa', 'gx', 'gy')
- residual_x: float32 [16, 4, 1024], P(None, 'pa', 'gy')
- residual_y: float32 [16, 4, 2048], P(None, 'pa', 'gx')
The draws below stay inside these ranges and needn't reach their ends.
Inputs may be any that keep to these rules, and one draw needn't show every extreme that they name: `view_slopes`: row 0 holds the near-x slopes in units of 1/512, row 1 the near-y slopes in units of 1/256; in each row both 14 and its negative occur.
All inputs are finite; a program needn't handle non-finite values.
Results may differ from the reference program's by a relative error of at most 0.0025.
Values may be sent and summed in bfloat16 or wider, within the bound.
A program may use at most 128 MiB of HBM per device.

```python
import jax
import jax.numpy as jnp
from jax import lax

CX = 512
CY = 256
VIEWS = 16
SHEAR = 14
HALO = 30
NX = 2048
NY = 1024
PLANES = 4


def draw_view_slopes(key, part):
    slopes = jax.random.randint(jax.random.fold_in(key, 11), (2, VIEWS), -SHEAR, SHEAR + 1, dtype=jnp.int32)
    for family in range(2):
        ranking = jax.random.permutation(jax.random.fold_in(key, 21 + family), VIEWS)
        slopes = slopes.at[family, ranking[0]].set(SHEAR)
        slopes = slopes.at[family, ranking[1]].set(-SHEAR)
    return slopes


def block_scale(rng, extent, pieces, smallest, top_value):
    loudness, own = 1.0, jax.random.fold_in(rng, 6)
    for dim, parts in pieces:
        heights = jnp.exp(jax.random.uniform(jax.random.fold_in(own, dim), (parts,), jnp.float32, smallest / len(pieces), top_value / len(pieces)))
        loudness = loudness * jnp.repeat(heights, extent[dim] // parts).reshape([-1 if axis == dim else 1 for axis in range(len(extent))])
    return loudness


def scatter_about(stream_key, extent, scale, reach, cuts=(), kind=jnp.bfloat16):
    values = scale * jax.random.normal(stream_key, extent, jnp.float32)
    if cuts:
        values = values * block_scale(stream_key, extent, cuts, -0.22, 0.18)
    return jnp.clip(values, -reach, reach).astype(kind)


def setup_inputs(seed: int = 0) -> dict:
    key_list = jax.random.split(jax.random.key(seed), 5)
    return {
        "volume": scatter_about(key_list[0], (PLANES, NX, NY), 1.0, 6.0, ((0, 2), (1, 4), (2, 4))),
        "view_slopes": draw_view_slopes(jax.random.fold_in(key_list[4], 71), 0),
        "measured_x": scatter_about(key_list[2], (VIEWS, PLANES, NY), 1.0, 6.0, ((1, 2), (2, 4)), jnp.float32),
        "measured_y": scatter_about(key_list[3], (VIEWS, PLANES, NX), 1.0, 6.0, ((1, 2), (2, 4)), jnp.float32),
    }


def rounded(values):
    return lax.optimization_barrier(values.astype(jnp.bfloat16)).astype(jnp.float32)


def shear_weights(slopes, cells_all, cells_dev):
    positions = jnp.arange(cells_all, dtype=jnp.int32) - cells_all // 2
    product = slopes[:, None] * positions[None, :]
    shifts = jnp.floor_divide(product, cells_dev)
    fraction = (product - shifts * cells_dev).astype(jnp.float32) / cells_dev
    return shifts, rounded(1.0 - fraction), rounded(fraction)


def project(source, shifts, lower, upper):
    planes_all, sweep_count, bin_count = source.shape
    padded = jnp.pad(source, ((0, 0), (0, 0), (HALO, HALO)))

    def one_view(strip, shift, low_weight, high_weight):
        segment = lax.dynamic_slice_in_dim(strip, (shift + HALO).astype(jnp.int32), bin_count + 1, 1)
        return low_weight * segment[:, :bin_count] + high_weight * segment[:, 1:]

    def advance(totals, position):
        strip = lax.dynamic_index_in_dim(padded, position, 1, False).astype(jnp.float32)
        shift_now = lax.dynamic_index_in_dim(shifts, position, 1, False)
        low_now = lax.dynamic_index_in_dim(lower, position, 1, False)
        high_now = lax.dynamic_index_in_dim(upper, position, 1, False)
        terms = jax.vmap(one_view, in_axes=(None, 0, 0, 0))(strip, shift_now, low_now, high_now)
        return totals + terms, None

    start = jnp.zeros((shifts.shape[0], planes_all, bin_count), jnp.float32)
    totals, unused = lax.scan(advance, start, jnp.arange(sweep_count, dtype=jnp.int32))
    return totals


def backproject(residual, shifts, lower, upper):
    view_count, planes_all, bin_count = residual.shape
    sweep_count = shifts.shape[1]
    padded = jnp.pad(residual, ((0, 0), (0, 0), (HALO, HALO)))

    def one_view(strip, shift, low_weight, high_weight):
        segment = lax.dynamic_slice_in_dim(strip, (HALO - shift - 1).astype(jnp.int32), bin_count + 1, 1)
        return low_weight * segment[:, 1:] + high_weight * segment[:, :bin_count]

    def advance(dummy, position):
        shift_now = lax.dynamic_index_in_dim(shifts, position, 1, False)
        low_now = lax.dynamic_index_in_dim(lower, position, 1, False)
        high_now = lax.dynamic_index_in_dim(upper, position, 1, False)
        terms = jax.vmap(one_view, in_axes=(0, 0, 0, 0))(padded, shift_now, low_now, high_now)
        return dummy, jnp.sum(terms, axis=0)

    dummy, stacked = lax.scan(advance, jnp.zeros((), jnp.float32), jnp.arange(sweep_count, dtype=jnp.int32))
    return jnp.moveaxis(stacked, 0, 1)


def reference(volume, view_slopes, measured_x, measured_y):
    shift_x, lower_x, upper_x = shear_weights(view_slopes[0], NX, CX)
    shift_y, lower_y, upper_y = shear_weights(view_slopes[1], NY, CY)
    scale_x = float(NX) ** -0.5
    scale_y = float(NY) ** -0.5
    forward_x = project(volume, shift_x, lower_x, upper_x) * scale_x
    forward_y = project(jnp.swapaxes(volume, 1, 2), shift_y, lower_y, upper_y) * scale_y
    residual_x = forward_x - measured_x
    residual_y = forward_y - measured_y
    back_x = backproject(rounded(residual_x), shift_x, lower_x, upper_x) * scale_x
    back_y = jnp.swapaxes(backproject(rounded(residual_y), shift_y, lower_y, upper_y), 1, 2) * scale_y
    values = volume.astype(jnp.float32)
    stacked = jnp.pad(values, ((1, 1), (0, 0), (0, 0)))
    coupling = 0.02 * (2.0 * values - stacked[:-2] - stacked[2:])
    gradient = back_x + back_y + coupling
    return gradient, residual_x, residual_y
```

```python
import functools

import jax
import jax.numpy as jnp
from jax import lax
from jax.experimental import pallas as pl
from jax.experimental.pallas import tpu as pltpu
from jax.sharding import PartitionSpec as P

SHEAR = 14
LEVELS = SHEAR + 2
VIEWS = 16
TILE = 128
MESH = pl.DeviceIdType.MESH


def slope_rows(slopes_ref, family):
    rows = lax.broadcasted_iota(jnp.int32, (VIEWS, TILE), 0)
    slopes = jnp.zeros((VIEWS, TILE), jnp.int32)
    for view in range(VIEWS):
        slopes = jnp.where(rows == view, slopes_ref[family, view], slopes)
    return slopes


def wide(tile, width):
    return jnp.concatenate([tile] * (width // TILE), axis=1)


def fill_table(table_ref, slopes, cells):
    position = lax.broadcasted_iota(jnp.int32, (VIEWS, cells), 1)
    slope = wide(slopes, cells)
    place = (slope * position - cells * jnp.minimum(slope, 0)).astype(jnp.float32) * (1.0 / cells)
    for level in range(LEVELS):
        weight = jnp.maximum(1.0 - jnp.abs(place - float(level)), 0.0)
        table_ref[level * VIEWS : (level + 1) * VIEWS, :] = weight.astype(jnp.bfloat16)


def leftward(value, amount):
    width = value.shape[1]
    return value if amount % width == 0 else pltpu.roll(value, (width - amount) % width, 1)


def shear_sum(summands, cells, fixed, amount, bits):
    ring = cells + TILE
    blank = jnp.zeros((VIEWS, TILE), jnp.float32)
    parts = [
        jnp.concatenate([summands[s * VIEWS : (s + 1) * VIEWS, :], blank], axis=1)
        for s in range(LEVELS)
    ]
    step = 1
    while len(parts) > 1:
        parts = [a + leftward(b, step) for a, b in zip(parts[::2], parts[1::2])]
        step *= 2
    around = leftward(parts[0], fixed)
    line = jnp.concatenate([around[:, cells:], around[:, :cells], blank], axis=1)
    amounts = wide(amount, cells + 2 * TILE)
    for bit in range(bits):
        chosen = (amounts & (1 << bit)) != 0
        line = jnp.where(chosen, pltpu.roll(line, 1 << bit, 1), line)
    return line


def spread(bins, cells, fixed, amount, bits, out_ref):
    amounts = wide(amount, cells + 2 * TILE)
    for bit in range(bits):
        chosen = (amounts & (1 << bit)) != 0
        bins = jnp.where(chosen, leftward(bins, 1 << bit), bins)
    bins = bins[:, : cells + TILE]
    for level in range(LEVELS):
        moved = pltpu.roll(bins, level + fixed, 1)[:, TILE:]
        out_ref[level * VIEWS : (level + 1) * VIEWS, :] = moved.astype(jnp.bfloat16)


class Family:
    def __init__(self, along, across, n_along, n_across, cells_along, cells, index, refs):
        self.along, self.across = along, across
        self.n, self.m = n_along, n_across
        self.cells_along, self.cells = cells_along, cells
        self.index = index
        self.me, self.place = lax.axis_index(along), lax.axis_index(across)
        self.fixed = SHEAR * (n_along // 2 - 1)
        self.bits = (SHEAR * (n_along - 1)).bit_length()
        self.scale = float(cells_along * n_along) ** -0.5
        (self.table, self.part, self.own, self.left, self.right, self.res, self.spread,
         self.send_sem, self.recv_sem) = refs

    def prepare(self, slopes_ref):
        slopes = slope_rows(slopes_ref, self.index)
        self.amount = self.fixed - slopes * (self.me - self.n // 2) - jnp.minimum(slopes, 0)
        fill_table(self.table, slopes, self.cells_along)

    def forward(self, volume_ref, measured_ref):
        planes = volume_ref.shape[0]
        chunk = self.part.shape[1]
        per = VIEWS // chunk
        for p in range(planes):
            dims = ((1,), (0,)) if self.index == 0 else ((1,), (1,))
            summands = lax.dot_general(
                self.table[...], volume_ref[p], (dims, ((), ())), preferred_element_type=jnp.float32
            )
            line = shear_sum(summands, self.cells, self.fixed, self.amount, self.bits) * self.scale
            measured = measured_ref[:, p, :]
            for c in range(per):
                slot = p * per + c
                piece = line[c * chunk : (c + 1) * chunk]
                mine = jnp.where(self.me == slot, measured[c * chunk : (c + 1) * chunk], 0.0)
                self.part[slot, :, :TILE] = piece[:, :TILE]
                self.part[slot, :, TILE : TILE + self.cells] = piece[:, TILE : TILE + self.cells] - mine
                self.part[slot, :, TILE + self.cells :] = piece[:, TILE + self.cells :]

    def copy(self, src, dst, kind, device):
        return pltpu.make_async_remote_copy(
            src_ref=src, dst_ref=dst, send_sem=self.send_sem.at[kind], recv_sem=self.recv_sem.at[kind],
            device_id=device, device_id_type=MESH,
        )

    def scatter(self):
        cells = self.cells
        for d in range(1, self.n):
            to = lax.rem(self.me + d, self.n)
            self.copy(self.part.at[to], self.own.at[d - 1], 0, {self.along: to}).start()

        @pl.when(self.place < self.m - 1)
        def _():
            for d in range(self.n):
                to = lax.rem(self.me + d, self.n)
                self.copy(
                    self.part.at[to, :, pl.ds(cells, 2 * TILE)], self.left.at[d], 1,
                    {self.along: to, self.across: self.place + 1},
                ).start()

        @pl.when(self.place > 0)
        def _():
            for d in range(self.n):
                to = lax.rem(self.me + d, self.n)
                self.copy(
                    self.part.at[to, :, pl.ds(0, 2 * TILE)], self.right.at[d], 2,
                    {self.along: to, self.across: self.place - 1},
                ).start()

    def nobody(self):
        return {self.along: lax.rem(self.me + 1, self.n)}

    def gather(self):
        cells = self.cells
        self.copy(self.own, self.own, 0, self.nobody()).wait_recv()
        self.res[self.me] = self.part[self.me] + functools.reduce(
            lambda a, b: a + b, [self.own[d] for d in range(self.n - 1)]
        )

        @pl.when(self.place > 0)
        def _():
            self.copy(self.left, self.left, 1, self.nobody()).wait_recv()
            total = functools.reduce(lambda a, b: a + b, [self.left[d] for d in range(self.n)])
            self.res[self.me, :, : 2 * TILE] += total

        @pl.when(self.place < self.m - 1)
        def _():
            self.copy(self.right, self.right, 2, self.nobody()).wait_recv()
            total = functools.reduce(lambda a, b: a + b, [self.right[d] for d in range(self.n)])
            self.res[self.me, :, cells : cells + 2 * TILE] += total

        for d in range(1, self.n):
            to = lax.rem(self.me + d, self.n)
            self.copy(self.res.at[self.me], self.res.at[self.me], 3, {self.along: to}).start()

    def backward(self, out_ref):
        cells = self.cells
        chunk = self.part.shape[1]
        per = VIEWS // chunk
        rest = self.res.at[pl.ds(0, self.n - 1)]
        self.copy(rest, rest, 3, self.nobody()).wait_recv()
        lane = lax.broadcasted_iota(jnp.int32, (VIEWS, cells + 2 * TILE), 1)
        first = jnp.where(self.place == 0, TILE, 0)
        end = jnp.where(self.place == self.m - 1, TILE + cells, cells + 2 * TILE)
        inside = (lane >= first) & (lane < end)
        for p in range(out_ref.shape[1]):
            bins = jnp.concatenate([self.res[p * per + c] for c in range(per)], axis=0)
            out_ref[:, p, :] = bins[:, TILE : TILE + cells]
            bins = jnp.where(inside, bins, 0.0)
            spread(bins, cells, self.fixed, self.amount, self.bits, self.spread.at[p])

    def finish(self):
        self.copy(self.own, self.own, 0, self.nobody()).wait_send()

        @pl.when(self.place < self.m - 1)
        def _():
            self.copy(self.left, self.left, 1, self.nobody()).wait_send()

        @pl.when(self.place > 0)
        def _():
            self.copy(self.right, self.right, 2, self.nobody()).wait_send()

        rest = self.res.at[pl.ds(0, self.n - 1)]
        self.copy(rest, rest, 3, self.nobody()).wait_send()


def kernel(sizes, volume, slopes, measured_x, measured_y, gradient, residual_x, residual_y, *scratch):
    nx, ny, npa = sizes
    planes, cells_x, cells_y = volume.shape
    fx = Family("gx", "gy", nx, ny, cells_x, cells_y, 0, scratch[0:9])
    fy = Family("gy", "gx", ny, nx, cells_y, cells_x, 1, scratch[9:18])
    before, after, plane_send, plane_recv = scratch[18:]
    i, j, k = lax.axis_index("gx"), lax.axis_index("gy"), lax.axis_index("pa")

    barrier = pltpu.get_barrier_semaphore()
    for di in range(nx):
        for dj in range(ny):
            if di or dj:
                pl.semaphore_signal(
                    barrier, inc=1, device_id_type=MESH,
                    device_id={"gx": lax.rem(i + di, nx), "gy": lax.rem(j + dj, ny)},
                )

    @pl.when(k > 0)
    def _():
        pl.semaphore_signal(barrier, inc=1, device_id={"pa": k - 1}, device_id_type=MESH)

    @pl.when(k < npa - 1)
    def _():
        pl.semaphore_signal(barrier, inc=1, device_id={"pa": k + 1}, device_id_type=MESH)

    fy.prepare(slopes)
    fx.prepare(slopes)
    count = nx * ny - 1 + jnp.where(k > 0, 1, 0) + jnp.where(k < npa - 1, 1, 0)
    pl.semaphore_wait(barrier, count)

    def up():
        return pltpu.make_async_remote_copy(
            src_ref=volume.at[planes - 1], dst_ref=before, send_sem=plane_send.at[0],
            recv_sem=plane_recv.at[0], device_id={"pa": lax.rem(k + 1, npa)}, device_id_type=MESH,
        )

    def down():
        return pltpu.make_async_remote_copy(
            src_ref=volume.at[0], dst_ref=after, send_sem=plane_send.at[1],
            recv_sem=plane_recv.at[1], device_id={"pa": lax.rem(k + npa - 1, npa)}, device_id_type=MESH,
        )

    @pl.when(k < npa - 1)
    def _():
        up().start()

    @pl.when(k > 0)
    def _():
        down().start()

    fy.forward(volume, measured_y)
    fy.scatter()
    fx.forward(volume, measured_x)
    fx.scatter()
    fy.gather()
    fx.gather()
    fy.backward(residual_y)
    tn = (((0,), (0,)), ((), ()))
    for p in range(planes):
        gradient[p] = fy.scale * lax.dot_general(
            fy.spread[p], fy.table[...], tn, preferred_element_type=jnp.float32
        )
    fx.backward(residual_x)

    @pl.when(k > 0)
    def _():
        up().wait_recv()

    @pl.when(k == 0)
    def _():
        before[...] = jnp.zeros_like(before)

    @pl.when(k < npa - 1)
    def _():
        down().wait_recv()

    @pl.when(k == npa - 1)
    def _():
        after[...] = jnp.zeros_like(after)

    for p in range(planes):
        low = (before[...] if p == 0 else volume[p - 1]).astype(jnp.float32)
        high = (after[...] if p == planes - 1 else volume[p + 1]).astype(jnp.float32)
        coupling = 0.02 * (2.0 * volume[p].astype(jnp.float32) - low - high)
        gradient[p] += coupling + fx.scale * lax.dot_general(
            fx.table[...], fx.spread[p], tn, preferred_element_type=jnp.float32
        )

    fy.finish()
    fx.finish()

    @pl.when(k < npa - 1)
    def _():
        up().wait_send()

    @pl.when(k > 0)
    def _():
        down().wait_send()


def family_scratch(n, planes, cells_along, cells):
    rows = planes * VIEWS // n
    return [
        pltpu.VMEM((LEVELS * VIEWS, cells_along), jnp.bfloat16),
        pltpu.VMEM((n, rows, cells + 2 * TILE), jnp.float32),
        pltpu.VMEM((n - 1, rows, cells + 2 * TILE), jnp.float32),
        pltpu.VMEM((n, rows, 2 * TILE), jnp.float32),
        pltpu.VMEM((n, rows, 2 * TILE), jnp.float32),
        pltpu.VMEM((n, rows, cells + 2 * TILE), jnp.float32),
        pltpu.VMEM((planes, LEVELS * VIEWS, cells), jnp.bfloat16),
        pltpu.SemaphoreType.DMA((4,)),
        pltpu.SemaphoreType.DMA((4,)),
    ]


def on_device(sizes, volume, view_slopes, measured_x, measured_y):
    nx, ny, _ = sizes
    planes, cells_x, cells_y = volume.shape
    vmem = pl.BlockSpec(memory_space=pltpu.VMEM)
    return pl.pallas_call(
        functools.partial(kernel, sizes),
        out_shape=(
            jax.ShapeDtypeStruct(volume.shape, jnp.float32),
            jax.ShapeDtypeStruct(measured_x.shape, jnp.float32),
            jax.ShapeDtypeStruct(measured_y.shape, jnp.float32),
        ),
        in_specs=[vmem, pl.BlockSpec(memory_space=pltpu.SMEM), vmem, vmem],
        out_specs=(vmem, vmem, vmem),
        scratch_shapes=[
            *family_scratch(nx, planes, cells_x, cells_y),
            *family_scratch(ny, planes, cells_y, cells_x),
            pltpu.VMEM((cells_x, cells_y), jnp.bfloat16),
            pltpu.VMEM((cells_x, cells_y), jnp.bfloat16),
            pltpu.SemaphoreType.DMA((2,)),
            pltpu.SemaphoreType.DMA((2,)),
        ],
        compiler_params=pltpu.CompilerParams(
            collective_id=0, has_side_effects=True, vmem_limit_bytes=32 * 2**20
        ),
    )(volume, view_slopes, measured_x, measured_y)


def solution(mesh):
    sizes = tuple(mesh.shape[name] for name in ("gx", "gy", "pa"))
    return jax.shard_map(
        functools.partial(on_device, sizes),
        mesh=mesh,
        in_specs=(P("pa", "gx", "gy"), P(), P(None, "pa", "gy"), P(None, "pa", "gx")),
        out_specs=(P("pa", "gx", "gy"), P(None, "pa", "gy"), P(None, "pa", "gx")),
        check_vma=False,
    )
```

```python
import functools

import jax
import jax.numpy as jnp
from jax import lax
from jax.experimental import pallas as pl
from jax.experimental.pallas import tpu as pltpu
from jax.sharding import PartitionSpec as P

SHEAR = 14
LEVELS = SHEAR + 2
VIEWS = 16
TILE = 128
MESH = pl.DeviceIdType.MESH


def slope_rows(slopes_ref, family):
    rows = lax.broadcasted_iota(jnp.int32, (VIEWS, TILE), 0)
    slopes = jnp.zeros((VIEWS, TILE), jnp.int32)
    for view in range(VIEWS):
        slopes = jnp.where(rows == view, slopes_ref[family, view], slopes)
    return slopes


def wide(tile, width):
    return jnp.concatenate([tile] * (width // TILE), axis=1)


def fill_table(table_ref, slopes, cells):
    position = lax.broadcasted_iota(jnp.int32, (VIEWS, cells), 1)
    slope = wide(slopes, cells)
    place = (slope * position - cells * jnp.minimum(slope, 0)).astype(jnp.float32) * (1.0 / cells)
    for level in range(LEVELS):
        weight = jnp.maximum(1.0 - jnp.abs(place - float(level)), 0.0)
        table_ref[level * VIEWS : (level + 1) * VIEWS, :] = weight.astype(jnp.bfloat16)


def leftward(value, amount):
    width = value.shape[1]
    return value if amount % width == 0 else pltpu.roll(value, (width - amount) % width, 1)


def shear_sum(summands, cells, fixed, amount, bits):
    ring = cells + TILE
    blank = jnp.zeros((VIEWS, TILE), jnp.float32)
    parts = [
        jnp.concatenate([summands[s * VIEWS : (s + 1) * VIEWS, :], blank], axis=1)
        for s in range(LEVELS)
    ]
    step = 1
    while len(parts) > 1:
        parts = [a + leftward(b, step) for a, b in zip(parts[::2], parts[1::2])]
        step *= 2
    around = leftward(parts[0], fixed)
    line = jnp.concatenate([around[:, cells:], around[:, :cells], blank], axis=1)
    amounts = wide(amount, cells + 2 * TILE)
    for bit in range(bits):
        chosen = (amounts & (1 << bit)) != 0
        line = jnp.where(chosen, pltpu.roll(line, 1 << bit, 1), line)
    return line


def spread(bins, cells, fixed, amount, bits, out_ref):
    amounts = wide(amount, cells + 2 * TILE)
    for bit in range(bits):
        chosen = (amounts & (1 << bit)) != 0
        bins = jnp.where(chosen, leftward(bins, 1 << bit), bins)
    bins = bins[:, : cells + TILE]
    for level in range(LEVELS):
        moved = pltpu.roll(bins, level + fixed, 1)[:, TILE:]
        out_ref[level * VIEWS : (level + 1) * VIEWS, :] = moved.astype(jnp.bfloat16)


class Family:
    def __init__(self, along, across, n_along, n_across, cells_along, cells, index, refs):
        self.along, self.across = along, across
        self.n, self.m = n_along, n_across
        self.cells_along, self.cells = cells_along, cells
        self.index = index
        self.me, self.place = lax.axis_index(along), lax.axis_index(across)
        self.fixed = SHEAR * (n_along // 2 - 1)
        self.bits = (SHEAR * (n_along - 1)).bit_length()
        self.scale = float(cells_along * n_along) ** -0.5
        (self.table, self.spread, self.part, self.own, self.left, self.right, self.res,
         self.send_sem, self.recv_sem) = refs

    def prepare(self, slopes_ref):
        slopes = slope_rows(slopes_ref, self.index)
        self.amount = self.fixed - slopes * (self.me - self.n // 2) - jnp.minimum(slopes, 0)
        fill_table(self.table, slopes, self.cells_along)

    def forward(self, volume_ref, measured_ref):
        planes = volume_ref.shape[0]
        chunk = self.part.shape[1]
        per = VIEWS // chunk
        for p in range(planes):
            dims = ((1,), (0,)) if self.index == 0 else ((1,), (1,))
            summands = lax.dot_general(
                self.table[...], volume_ref[p], (dims, ((), ())), preferred_element_type=jnp.float32
            )
            line = shear_sum(summands, self.cells, self.fixed, self.amount, self.bits) * self.scale
            measured = measured_ref[:, p, :]
            for c in range(per):
                slot = p * per + c
                piece = line[c * chunk : (c + 1) * chunk]
                mine = jnp.where(self.me == slot, measured[c * chunk : (c + 1) * chunk], 0.0)
                self.part[slot, :, :TILE] = piece[:, :TILE]
                self.part[slot, :, TILE : TILE + self.cells] = piece[:, TILE : TILE + self.cells] - mine
                self.part[slot, :, TILE + self.cells :] = piece[:, TILE + self.cells :]

    def copy(self, src, dst, kind, device):
        return pltpu.make_async_remote_copy(
            src_ref=src, dst_ref=dst, send_sem=self.send_sem.at[kind], recv_sem=self.recv_sem.at[kind],
            device_id=device, device_id_type=MESH,
        )

    def scatter(self):
        cells = self.cells
        for d in range(1, self.n):
            to = lax.rem(self.me + d, self.n)
            self.copy(self.part.at[to], self.own.at[d - 1], 0, {self.along: to}).start()

        @pl.when(self.place < self.m - 1)
        def _():
            for d in range(self.n):
                to = lax.rem(self.me + d, self.n)
                self.copy(
                    self.part.at[to, :, pl.ds(cells, 2 * TILE)], self.left.at[d], 1,
                    {self.along: to, self.across: self.place + 1},
                ).start()

        @pl.when(self.place > 0)
        def _():
            for d in range(self.n):
                to = lax.rem(self.me + d, self.n)
                self.copy(
                    self.part.at[to, :, pl.ds(0, 2 * TILE)], self.right.at[d], 2,
                    {self.along: to, self.across: self.place - 1},
                ).start()

    def nobody(self):
        return {self.along: lax.rem(self.me + 1, self.n)}

    def gather(self):
        cells = self.cells
        self.copy(self.own, self.own, 0, self.nobody()).wait_recv()
        self.res[self.me] = self.part[self.me] + functools.reduce(
            lambda a, b: a + b, [self.own[d] for d in range(self.n - 1)]
        )

        @pl.when(self.place > 0)
        def _():
            self.copy(self.left, self.left, 1, self.nobody()).wait_recv()
            total = functools.reduce(lambda a, b: a + b, [self.left[d] for d in range(self.n)])
            self.res[self.me, :, : 2 * TILE] += total

        @pl.when(self.place < self.m - 1)
        def _():
            self.copy(self.right, self.right, 2, self.nobody()).wait_recv()
            total = functools.reduce(lambda a, b: a + b, [self.right[d] for d in range(self.n)])
            self.res[self.me, :, cells : cells + 2 * TILE] += total

        for d in range(1, self.n):
            to = lax.rem(self.me + d, self.n)
            self.copy(self.res.at[self.me], self.res.at[self.me], 3, {self.along: to}).start()

    def backward(self, out_ref):
        cells = self.cells
        chunk = self.part.shape[1]
        per = VIEWS // chunk
        rest = self.res.at[pl.ds(0, self.n - 1)]
        self.copy(rest, rest, 3, self.nobody()).wait_recv()
        lane = lax.broadcasted_iota(jnp.int32, (VIEWS, cells + 2 * TILE), 1)
        first = jnp.where(self.place == 0, TILE, 0)
        end = jnp.where(self.place == self.m - 1, TILE + cells, cells + 2 * TILE)
        inside = (lane >= first) & (lane < end)
        for p in range(out_ref.shape[1]):
            bins = jnp.concatenate([self.res[p * per + c] for c in range(per)], axis=0)
            out_ref[:, p, :] = bins[:, TILE : TILE + cells]
            bins = jnp.where(inside, bins, 0.0)
            spread(bins, cells, self.fixed, self.amount, self.bits, self.spread.at[p])

    def finish(self):
        self.copy(self.own, self.own, 0, self.nobody()).wait_send()

        @pl.when(self.place < self.m - 1)
        def _():
            self.copy(self.left, self.left, 1, self.nobody()).wait_send()

        @pl.when(self.place > 0)
        def _():
            self.copy(self.right, self.right, 2, self.nobody()).wait_send()

        rest = self.res.at[pl.ds(0, self.n - 1)]
        self.copy(rest, rest, 3, self.nobody()).wait_send()


def exchange(sizes, volume_hbm, slopes_hbm, measured_x_hbm, measured_y_hbm, residual_x, residual_y,
             table_x, table_y, spread_x, spread_y, volume, before, after, *scratch):
    nx, ny, npa = sizes
    planes, cells_x, cells_y = volume.shape
    fx = Family("gx", "gy", nx, ny, cells_x, cells_y, 0, (table_x, spread_x, *scratch[0:7]))
    fy = Family("gy", "gx", ny, nx, cells_y, cells_x, 1, (table_y, spread_y, *scratch[7:14]))
    slopes, measured_x, measured_y, plane_send, plane_recv, load_sem = scratch[14:]
    i, j, k = lax.axis_index("gx"), lax.axis_index("gy"), lax.axis_index("pa")

    load_slopes = pltpu.make_async_copy(slopes_hbm, slopes, load_sem.at[0])
    load_volume = pltpu.make_async_copy(volume_hbm, volume, load_sem.at[1])
    load_x = pltpu.make_async_copy(measured_x_hbm, measured_x, load_sem.at[2])
    load_y = pltpu.make_async_copy(measured_y_hbm, measured_y, load_sem.at[3])
    for load in (load_slopes, load_volume, load_y, load_x):
        load.start()

    barrier = pltpu.get_barrier_semaphore()
    for di in range(nx):
        for dj in range(ny):
            if di or dj:
                pl.semaphore_signal(
                    barrier, inc=1, device_id_type=MESH,
                    device_id={"gx": lax.rem(i + di, nx), "gy": lax.rem(j + dj, ny)},
                )

    @pl.when(k > 0)
    def _():
        pl.semaphore_signal(barrier, inc=1, device_id={"pa": k - 1}, device_id_type=MESH)

    @pl.when(k < npa - 1)
    def _():
        pl.semaphore_signal(barrier, inc=1, device_id={"pa": k + 1}, device_id_type=MESH)

    load_slopes.wait()
    fy.prepare(slopes)
    fx.prepare(slopes)
    load_volume.wait()
    count = nx * ny - 1 + jnp.where(k > 0, 1, 0) + jnp.where(k < npa - 1, 1, 0)
    pl.semaphore_wait(barrier, count)

    def up():
        return pltpu.make_async_remote_copy(
            src_ref=volume.at[planes - 1], dst_ref=before, send_sem=plane_send.at[0],
            recv_sem=plane_recv.at[0], device_id={"pa": lax.rem(k + 1, npa)}, device_id_type=MESH,
        )

    def down():
        return pltpu.make_async_remote_copy(
            src_ref=volume.at[0], dst_ref=after, send_sem=plane_send.at[1],
            recv_sem=plane_recv.at[1], device_id={"pa": lax.rem(k + npa - 1, npa)}, device_id_type=MESH,
        )

    @pl.when(k < npa - 1)
    def _():
        up().start()

    @pl.when(k > 0)
    def _():
        down().start()

    load_y.wait()
    fy.forward(volume, measured_y)
    fy.scatter()
    load_x.wait()
    fx.forward(volume, measured_x)
    fx.scatter()
    fy.gather()
    fx.gather()
    fy.backward(residual_y)
    fx.backward(residual_x)

    @pl.when(k > 0)
    def _():
        up().wait_recv()

    @pl.when(k == 0)
    def _():
        before[...] = jnp.zeros_like(before)

    @pl.when(k < npa - 1)
    def _():
        down().wait_recv()

    @pl.when(k == npa - 1)
    def _():
        after[...] = jnp.zeros_like(after)

    fy.finish()
    fx.finish()

    @pl.when(k < npa - 1)
    def _():
        up().wait_send()

    @pl.when(k > 0)
    def _():
        down().wait_send()


def combine(scale_x, scale_y, residual_x, residual_y, table_x, table_y, spread_x, spread_y, volume, before, after,
            gradient_hbm, residual_x_hbm, residual_y_hbm, gradient, sem):
    planes, cells_x, _ = volume.shape
    stores = [
        pltpu.make_async_copy(residual_x, residual_x_hbm, sem.at[0]),
        pltpu.make_async_copy(residual_y, residual_y_hbm, sem.at[1]),
    ]
    for store in stores:
        store.start()
    tn = (((0,), (0,)), ((), ()))
    half = cells_x // 2
    for p in range(planes):
        for h in range(2):
            rows = pl.ds(h * half, half)
            low = (before[rows] if p == 0 else volume[p - 1, rows]).astype(jnp.float32)
            high = (after[rows] if p == planes - 1 else volume[p + 1, rows]).astype(jnp.float32)
            coupling = 0.02 * (2.0 * volume[p, rows].astype(jnp.float32) - low - high)
            back_x = lax.dot_general(table_x[:, rows], spread_x[p], tn, preferred_element_type=jnp.float32)
            back_y = lax.dot_general(spread_y[p, :, rows], table_y[...], tn, preferred_element_type=jnp.float32)
            gradient[p, rows] = scale_x * back_x + scale_y * back_y + coupling
            store = pltpu.make_async_copy(
                gradient.at[p, rows], gradient_hbm.at[p, rows], sem.at[2 + 2 * p + h]
            )
            store.start()
            stores.append(store)
    for store in stores:
        store.wait()


def family_scratch(n, planes, cells):
    rows = planes * VIEWS // n
    return [
        pltpu.VMEM((n, rows, cells + 2 * TILE), jnp.float32),
        pltpu.VMEM((n - 1, rows, cells + 2 * TILE), jnp.float32),
        pltpu.VMEM((n, rows, 2 * TILE), jnp.float32),
        pltpu.VMEM((n, rows, 2 * TILE), jnp.float32),
        pltpu.VMEM((n, rows, cells + 2 * TILE), jnp.float32),
        pltpu.SemaphoreType.DMA((4,)),
        pltpu.SemaphoreType.DMA((4,)),
    ]


def on_device(sizes, volume, view_slopes, measured_x, measured_y):
    nx, ny, _ = sizes
    planes, cells_x, cells_y = volume.shape
    vmem = pl.BlockSpec(memory_space=pltpu.VMEM)
    hbm = pl.BlockSpec(memory_space=pltpu.HBM)
    shape = jax.ShapeDtypeStruct
    rows = LEVELS * VIEWS
    held = pl.pallas_call(
        functools.partial(exchange, sizes),
        out_shape=(
            shape(measured_x.shape, jnp.float32),
            shape(measured_y.shape, jnp.float32),
            shape((rows, cells_x), jnp.bfloat16),
            shape((rows, cells_y), jnp.bfloat16),
            shape((planes, rows, cells_y), jnp.bfloat16),
            shape((planes, rows, cells_x), jnp.bfloat16),
            shape(volume.shape, jnp.bfloat16),
            shape((cells_x, cells_y), jnp.bfloat16),
            shape((cells_x, cells_y), jnp.bfloat16),
        ),
        in_specs=[hbm] * 4,
        out_specs=(vmem,) * 9,
        scratch_shapes=[
            *family_scratch(nx, planes, cells_y),
            *family_scratch(ny, planes, cells_x),
            pltpu.SMEM(view_slopes.shape, jnp.int32),
            pltpu.VMEM(measured_x.shape, jnp.float32),
            pltpu.VMEM(measured_y.shape, jnp.float32),
            pltpu.SemaphoreType.DMA((2,)),
            pltpu.SemaphoreType.DMA((2,)),
            pltpu.SemaphoreType.DMA((4,)),
        ],
        compiler_params=pltpu.CompilerParams(
            collective_id=0, has_side_effects=True, vmem_limit_bytes=24 * 2**20
        ),
    )(volume, view_slopes, measured_x, measured_y)
    scale_x = float(cells_x * nx) ** -0.5
    scale_y = float(cells_y * ny) ** -0.5
    return pl.pallas_call(
        functools.partial(combine, scale_x, scale_y),
        out_shape=(
            shape(volume.shape, jnp.float32),
            shape(measured_x.shape, jnp.float32),
            shape(measured_y.shape, jnp.float32),
        ),
        in_specs=[vmem] * 9,
        out_specs=(hbm,) * 3,
        scratch_shapes=[
            pltpu.VMEM(volume.shape, jnp.float32),
            pltpu.SemaphoreType.DMA((2 + 2 * planes,)),
        ],
        compiler_params=pltpu.CompilerParams(vmem_limit_bytes=24 * 2**20),
    )(*held)


def solution(mesh):
    sizes = tuple(mesh.shape[name] for name in ("gx", "gy", "pa"))
    return jax.shard_map(
        functools.partial(on_device, sizes),
        mesh=mesh,
        in_specs=(P("pa", "gx", "gy"), P(), P(None, "pa", "gy"), P(None, "pa", "gx")),
        out_specs=(P("pa", "gx", "gy"), P(None, "pa", "gy"), P(None, "pa", "gx")),
        check_vma=False,
    )
```
